32 devices in a mesh: groups: 2 (over y), pts: 4 (over z), blk: 2 (over x), rep: 2 (over core).
Axes of the slice: x: 2, y: 2, z: 4, core: 2. Of those that a mesh axis runs over, the one named last changes fastest.
Arguments:
- points_x: bfloat16 [32768, 512], P(('groups', 'pts', 'blk')), parts along dimension 0, may hold values from -6 to 6
- coords: float32 [3, 32768], P(None, ('groups', 'pts', 'blk')), parts along dimension 1, may hold values from 0 to 32
- panels: bfloat16 [32768, 256], P(('groups', 'pts', 'blk')), parts along dimension 0, may hold values from -0.09375 to 0.09375
- coupling: bfloat16 [2048, 256], P(('groups', 'pts')), parts along dimension 0, may hold values from -0.375 to 0.375
- near_list: int32 [64, 4], P(('groups', 'pts', 'blk')), parts along dimension 0, may hold values from -1 to 31, as said below
- order: int32 [32768], P(('groups', 'pts', 'blk')), parts along dimension 0, may hold values from 0 to 16383, as said below
Outputs:
- product: float32 [32768, 512], P(('groups', 'pts', 'blk', 'rep')), parts along dimension 0
The draws below stay inside these ranges and needn't reach their ends.
There are 2 independent parts, one for each index of `groups`. The reference program is written for one: setup_inputs(seed, part) draws one part's arguments, and reference() takes and returns one part's arrays. A program takes and returns all parts, laid end to end along the dimension named above; each array names one. Nothing has to cross between parts.
Inputs may be any that keep to these rules, and one draw needn't show every extreme that they name: `near_list`: each near-field entry is -1 or a leaf among the same 4 consecutive leaves (aligned) as its own leaf; slot 0 is the leaf itself; live entries of a row are distinct and come before empty ones; some leaf of every draw has all 4 slots live. `order`: each aligned block of 2048 tree positions holds a permutation of the same block of point indices.
All inputs are finite; a program needn't handle non-finite values.
Results may differ from the reference program's by a relative error of at most 0.00036.
Values sent between devices are 32-bit elements; how exact they have to be, the bound alone decides.
A program may use at most 64 MiB of HBM per device.

```python
import jax
import jax.numpy as jnp
from jax import lax

LEAF = 512
R = 256
NEAR = 4
NRHS = 512
LPD = 4
SEGMENTS = 4
LEVELS = 2
SEG_POINTS = 4096
N_LEAVES = 32
POINTS = 16384
COUPLE_ROWS = 1024
N_PTS = 4
N_BLK = 2


def shuffle_blocks(key):
    key = jax.random.fold_in(key, 23)
    blocks = N_PTS * N_BLK
    size = LPD * LEAF
    keys = jax.random.split(key, blocks)
    perms = jax.vmap(lambda k: jax.random.permutation(k, size))(keys).astype(jnp.int32)
    starts = (jnp.arange(blocks, dtype=jnp.int32) * size)[:, None]
    return (perms + starts).reshape(POINTS).astype(jnp.int32)


def draw_order(key, part):
    return shuffle_blocks(key)


def draw_coords(key, part):
    order = shuffle_blocks(key)
    key = jax.random.fold_in(key, 37)
    tree_pos = jnp.arange(POINTS, dtype=jnp.int32)
    leaf = tree_pos // LEAF
    group = leaf // LPD
    gx = (group % 8).astype(jnp.float32) * 4.0
    gy = (group // 8 % 8).astype(jnp.float32) * 4.0
    gz = (group // 64 % 8).astype(jnp.float32) * 4.0
    centers = jnp.stack([gx, gy, gz], axis=0)
    jitter = jax.random.uniform(key, (3, POINTS), jnp.float32, 0.0, 0.5)
    tree_coords = centers + jitter
    return jnp.zeros((3, POINTS), jnp.float32).at[:, order].set(tree_coords)


def draw_points_x(key, part):
    key = jax.random.fold_in(key, 53)
    key_noise, key_offset = jax.random.split(key, 2)
    offset = jax.random.uniform(key_offset, (NRHS,), jnp.float32, 0.6, 1.2)
    noise = jnp.clip(jax.random.normal(key_noise, (POINTS, NRHS), jnp.float32), -4.5, 4.5)
    return (noise + offset[None, :]).astype(jnp.bfloat16)


def draw_near_list(key, part):
    key = jax.random.fold_in(key, 11)
    key_perm, key_heavy, key_count = jax.random.split(key, 3)
    leaves = jnp.arange(N_LEAVES, dtype=jnp.int32)
    block_start = leaves // LPD * LPD
    local = leaves % LPD
    perm_keys = jax.random.split(key_perm, N_LEAVES)
    offsets = jax.vmap(lambda k: jax.random.permutation(k, LPD - 1))(perm_keys)[:, :NEAR - 1].astype(jnp.int32) + 1
    steps = jnp.concatenate([jnp.zeros((N_LEAVES, 1), jnp.int32), offsets], axis=1)
    ids = block_start[:, None] + (local[:, None] + steps) % LPD
    heavy = jax.random.randint(key_heavy, (N_LEAVES // LPD,), 0, 2)
    heavy = jnp.repeat(heavy, LPD)
    count = jax.random.randint(key_count, (N_LEAVES,), 1, NEAR + 1)
    count = jnp.where(heavy == 1, NEAR, count)
    count = count.at[0].set(NEAR)
    slots = jnp.arange(NEAR, dtype=jnp.int32)[None, :]
    return jnp.where(slots < count[:, None], ids, -1).astype(jnp.int32)


def steps_of(own_key, extent, shards, low, top_value):
    level = 1.0
    for axis_at, blocks in shards:
        steps = jax.random.uniform(jax.random.fold_in(jax.random.fold_in(own_key, 6), axis_at), (blocks,), jnp.float32, low / len(shards), top_value / len(shards))
        level = level * jnp.repeat(jnp.exp(steps), extent[axis_at] // blocks).reshape((-1,) + (1,) * (len(extent) - 1 - axis_at))
    return level


def normal_values(own_key, dims, scale, bound, cuts=(), kind=jnp.bfloat16):
    loudness = steps_of(own_key, dims, cuts, -0.22, 0.18) if cuts else 1.0
    array = jax.random.normal(own_key, dims, jnp.float32) * scale * loudness
    return jnp.minimum(jnp.maximum(array, -bound), bound).astype(kind)


def setup_inputs(seed: int = 0, part: int = 0) -> dict:
    seeds = jax.random.split(jax.random.key(seed), 7)
    part_splits = jax.random.split(jax.random.fold_in(seeds[6], part), 7)
    return {
        "points_x": draw_points_x(jax.random.fold_in(jax.random.fold_in(seeds[6], part), 71), part),
        "coords": draw_coords(jax.random.fold_in(jax.random.fold_in(seeds[6], part), 71), part),
        "panels": normal_values(part_splits[2], (POINTS, R), SEG_POINTS ** -0.5, 0.09375, ((0, 8),)),
        "coupling": normal_values(part_splits[3], (COUPLE_ROWS, R), R ** -0.5, 0.375, ((0, 4),)),
        "near_list": draw_near_list(jax.random.fold_in(jax.random.fold_in(seeds[6], part), 71), part),
        "order": draw_order(jax.random.fold_in(jax.random.fold_in(seeds[6], part), 71), part),
    }


spread = 1.0 / (2.0 * 0.1 * 0.1)


def kernel_block(left, right):
    gap = left[:, :, None] - right[:, None, :]
    dist = jnp.sum(gap * gap, axis=0)
    return jnp.exp(-dist * spread).astype(jnp.bfloat16)


def reference(points_x, coords, panels, coupling, near_list, order):
    tree_x = jnp.take(points_x, order, axis=0)
    tree_c = jnp.take(coords, order, axis=1)
    leaves_x = tree_x.reshape(N_LEAVES, LEAF, NRHS)
    leaves_c = tree_c.reshape(3, N_LEAVES, LEAF).transpose(1, 0, 2)

    def near_rows(leaf):
        total = jnp.zeros((LEAF, NRHS), jnp.float32)
        for slot in range(NEAR):
            ident = near_list[leaf, slot]
            other = jnp.maximum(ident, 0)
            block = kernel_block(leaves_c[leaf], leaves_c[other])
            term = jnp.dot(block, leaves_x[other], preferred_element_type=jnp.float32)
            total = total + jnp.where(ident >= 0, term, jnp.float32(0.0))
        return total

    near = lax.map(near_rows, jnp.arange(N_LEAVES, dtype=jnp.int32)).reshape(POINTS, NRHS)
    seg_x = tree_x.reshape(SEGMENTS, SEG_POINTS, NRHS)
    seg_p = panels.reshape(SEGMENTS, SEG_POINTS, R)

    def project(pair):
        return lax.dot_general(pair[0], pair[1], (((0,), (0,)), ((), ())), preferred_element_type=jnp.float32)

    coef = lax.map(project, (seg_p, seg_x))
    incoming = jnp.zeros((SEGMENTS, R, NRHS), jnp.float32)
    for bit in range(LEVELS):
        grouped = coef.reshape(SEGMENTS >> bit, 1 << bit, R, NRHS).sum(axis=1)
        swapped = grouped.reshape(-1, 2, R, NRHS)[:, ::-1].reshape(-1, R, NRHS)
        incoming = incoming + (2.0 ** (-0.5 * bit)) * jnp.repeat(swapped, 1 << bit, axis=0)
    mats = coupling.reshape(SEGMENTS, R, R).astype(jnp.float32)
    mixed = jnp.einsum("srk,skn->srn", mats, incoming, precision=lax.Precision.HIGHEST).astype(jnp.bfloat16)
    far = jnp.einsum("spr,srn->spn", seg_p.astype(jnp.float32), mixed.astype(jnp.float32), precision=lax.Precision.HIGHEST)
    far = far.reshape(POINTS, NRHS)
    return near * (LEAF ** -0.5) + far
```

```python
import functools

import jax
import jax.numpy as jnp
from jax import lax
from jax.experimental import pallas as pl
from jax.experimental.pallas import tpu as pltpu
from jax.sharding import PartitionSpec as P

LEAF = 512
LANES = 128
TILE = 256
SUB = 64
FAR_AWAY = 1e18
MESH = pl.DeviceIdType.MESH

spread = 1.0 / (2.0 * 0.1 * 0.1)


def nt_dot(left, right):
    return lax.dot_general(
        left, right, (((1,), (1,)), ((), ())), preferred_element_type=jnp.float32
    )


def tn_dot(left, right):
    return lax.dot_general(
        left, right, (((0,), (0,)), ((), ())), preferred_element_type=jnp.float32
    )


def prepare_kernel(
    order_row, order_tile, coords, near_list, panels, points_x, coef_out, p_out, q_out
):
    rows = points_x.shape[0]
    nrhs = points_x.shape[1]
    rep_count = lax.axis_size("rep")
    rep = lax.axis_index("rep")
    start = (lax.axis_index("pts") * lax.axis_size("blk") + lax.axis_index("blk")) * rows
    base_leaf = start // LEAF
    half = nrhs // rep_count
    own_rows = rows // rep_count
    groups = rows // LANES
    leaf_count = rows // LEAF
    own_leaves = leaf_count // rep_count

    local = order_row[...] - start
    high = lax.shift_right_logical(local, 8)
    low = (local & (TILE - 1)).astype(jnp.float32)
    columns = pl.ds(pl.multiple_of(rep * half, LANES), half)
    lane_at = lax.broadcasted_iota(jnp.int32, (TILE, rows), 0).astype(jnp.float32).astype(jnp.bfloat16)
    total = jnp.zeros(coef_out.shape, jnp.float32)
    for tile in range(rows // TILE):
        want = jnp.where(high == tile, low, -1.0).astype(jnp.bfloat16)
        chosen = jnp.where(lane_at == want, jnp.bfloat16(1), jnp.bfloat16(0))
        moved = jnp.dot(chosen, panels[...], preferred_element_type=jnp.float32)
        total = total + tn_dot(
            points_x[pl.ds(tile * TILE, TILE), columns], moved.astype(jnp.bfloat16)
        )
    coef_out[...] = total

    per_core = own_rows // LANES
    own = order_tile[pl.ds(pl.multiple_of(rep * per_core, 8), per_core), :] - start
    own_high = lax.shift_right_logical(own, 7)
    own_low = own & (LANES - 1)
    picked = []
    for axis in range(3):
        value = jnp.zeros((per_core, LANES), jnp.float32)
        for group in range(groups):
            source = jnp.broadcast_to(
                coords[axis : axis + 1, group * LANES : (group + 1) * LANES], (per_core, LANES)
            )
            got = jnp.take_along_axis(source, own_low, axis=1, mode="promise_in_bounds")
            value = jnp.where(own_high == group, got, value)
        picked.append(value)
    blank = jnp.zeros((5, LANES), jnp.float32)
    pieces = []
    for row in range(per_core):
        pieces += [value[row : row + 1] for value in picked] + [blank]
    stacked = jnp.concatenate(pieces + [jnp.zeros((LANES - 8 * per_core, LANES), jnp.float32)], axis=0)
    turned = stacked.T
    for row in range(per_core):
        p_out[row * LANES : (row + 1) * LANES, :] = turned[:, row * 8 : (row + 1) * 8]

    high7 = lax.shift_right_logical(local, 7)
    low7 = local & (LANES - 1)
    leaf_at = lax.broadcasted_iota(jnp.int32, (1, rows), 1) // LEAF
    key = leaf_at * groups + high7
    left = (lax.broadcasted_iota(jnp.int32, (leaf_count * groups, rows), 0) == key).astype(jnp.float32)
    right = (lax.broadcasted_iota(jnp.int32, (LANES, rows), 0) == low7).astype(jnp.float32)
    member = nt_dot(left.astype(jnp.bfloat16), right.astype(jnp.bfloat16))
    folded = [
        jnp.concatenate(
            [coords[axis : axis + 1, g * LANES : (g + 1) * LANES] for g in range(groups)], axis=0
        )
        for axis in range(3)
    ]
    for own_leaf in range(own_leaves):
        leaf = rep * own_leaves + own_leaf
        live = jnp.zeros((groups, LANES), jnp.float32)
        for other in range(leaf_count):
            hit = near_list[leaf, 0] == base_leaf + other
            for slot in range(1, near_list.shape[1]):
                hit = jnp.logical_or(hit, near_list[leaf, slot] == base_leaf + other)
            weight = jnp.where(hit, 1.0, 0.0)
            live = live + weight * member[other * groups : (other + 1) * groups]
        q_out[own_leaf * groups : (own_leaf + 1) * groups, :] = jnp.where(
            live > 0.5, folded[0], FAR_AWAY
        )
    for axis in (1, 2):
        at = (own_leaves + axis - 1) * groups
        q_out[at : at + groups, :] = folded[axis]


def exchange_kernel(
    levels,
    chunks,
    coef,
    coupling,
    p_cols,
    q_rows,
    x_hbm,
    near_hbm,
    mixed_out,
    x_buf,
    k_buf,
    near_buf,
    blk_buf,
    run_buf,
    pts_buf,
    inc_buf,
    gather_buf,
    x_sem,
    near_sem,
    blk_send,
    blk_recv,
    pts_send,
    pts_recv,
    all_send,
    all_recv,
    rep_send,
    rep_recv,
):
    blk_count = lax.axis_size("blk")
    rep_count = lax.axis_size("rep")
    rep = lax.axis_index("rep")
    blk = lax.axis_index("blk")
    seg = lax.axis_index("pts")
    half = coef.shape[0]
    piece = half // blk_count
    step = piece // chunks
    groups = x_buf.shape[0] // LANES
    own_rows = p_cols.shape[0]
    own_leaves = own_rows // LEAF

    x_copy = pltpu.make_async_copy(x_hbm, x_buf, x_sem)
    x_copy.start()

    def blk_peer(d):
        return lax.rem(blk + d, blk_count)

    def rep_peer(d):
        return lax.rem(rep + d, rep_count)

    def pts_peer(bit):
        mask = 2**bit
        return seg + mask - 2 * mask * lax.rem(lax.div(seg, mask), 2)

    peers = (
        [{"blk": blk_peer(d)} for d in range(1, blk_count)]
        + [{"rep": rep_peer(d)} for d in range(1, rep_count)]
        + [{"pts": pts_peer(bit)} for bit in range(levels)]
    )
    barrier = pltpu.get_barrier_semaphore()
    for peer in peers:
        pl.semaphore_signal(barrier, inc=1, device_id=peer, device_id_type=MESH)
    pl.semaphore_wait(barrier, len(peers))

    def remote(src, dst, send, recv, peer):
        return pltpu.make_async_remote_copy(
            src_ref=src, dst_ref=dst, send_sem=send, recv_sem=recv,
            device_id=peer, device_id_type=MESH,
        )

    def rows_of(first, chunk):
        return pl.ds(pl.multiple_of(first + chunk * step, 8), step)

    blk_copies = {}
    for chunk in range(chunks):
        for d in range(1, blk_count):
            other = blk_peer(d)
            copy = remote(
                coef.at[rows_of(other * piece, chunk)],
                blk_buf.at[d - 1, pl.ds(chunk * step, step)],
                blk_send.at[d - 1, chunk],
                blk_recv.at[d - 1, chunk],
                {"blk": other},
            )
            copy.start()
            blk_copies[d, chunk] = copy

    pts_copies = {}

    def start_level(bit, chunk):
        at = pl.ds(chunk * step, step)
        copy = remote(
            run_buf.at[bit, at],
            pts_buf.at[bit, at],
            pts_send.at[bit, chunk],
            pts_recv.at[bit, chunk],
            {"pts": pts_peer(bit)},
        )
        copy.start()
        pts_copies[bit, chunk] = copy

    def reduce_blk(chunk):
        at = pl.ds(chunk * step, step)
        value = coef[rows_of(blk * piece, chunk), :]
        for d in range(1, blk_count):
            blk_copies[d, chunk].wait_recv()
            value = value + blk_buf[d - 1, at, :]
        run_buf[0, at, :] = value
        if levels:
            start_level(0, chunk)
        else:
            inc_buf[at, :] = jnp.zeros_like(value)

    all_copies = {}
    rep_copies = {}

    def level(bit, chunk):
        at = pl.ds(chunk * step, step)
        pts_copies[bit, chunk].wait_recv()
        got = pts_buf[bit, at, :]
        if bit + 1 < levels:
            run_buf[bit + 1, at, :] = run_buf[bit, at, :] + got
            start_level(bit + 1, chunk)
        scaled = 2.0 ** (-0.5 * bit) * got
        inc_buf[at, :] = scaled if bit == 0 else inc_buf[at, :] + scaled

    def mix(chunk):
        at = pl.ds(chunk * step, step)
        value = inc_buf[at, :]
        top = value.astype(jnp.bfloat16)
        rest = value - top.astype(jnp.float32)
        middle = rest.astype(jnp.bfloat16)
        bottom = (rest - middle.astype(jnp.float32)).astype(jnp.bfloat16)
        mats = coupling[...]
        mixed = nt_dot(bottom, mats) + nt_dot(middle, mats) + nt_dot(top, mats)
        own = rows_of(rep * half + blk * piece, chunk)
        gather_buf[own, :] = mixed.astype(jnp.bfloat16).astype(jnp.float32)
        for d in range(1, blk_count):
            copy = remote(
                gather_buf.at[own], gather_buf.at[own],
                all_send.at[d - 1, chunk], all_recv.at[d - 1, chunk], {"blk": blk_peer(d)},
            )
            copy.start()
            all_copies[d, chunk] = copy
        pass_on(0, chunk)

    def pass_on(back, chunk):
        if back:
            all_copies[back, chunk].wait_recv()
        source = lax.rem(blk + blk_count - back, blk_count)
        at = rows_of(rep * half + source * piece, chunk)
        for d in range(1, rep_count):
            copy = remote(
                gather_buf.at[at], gather_buf.at[at],
                rep_send.at[d - 1, back, chunk], rep_recv.at[d - 1, back, chunk],
                {"rep": rep_peer(d)},
            )
            copy.start()
            rep_copies[d, back, chunk] = copy

    near_copies = []

    def near_tile(tile):
        leaf = tile * TILE // LEAF
        for sub in range(TILE // SUB):
            at = tile * TILE + sub * SUB
            left = [
                jnp.broadcast_to(p_cols[at : at + SUB, axis : axis + 1], (SUB, LANES))
                for axis in range(3)
            ]
            for group in range(groups):
                gx = left[0] - q_rows[leaf * groups + group : leaf * groups + group + 1, :]
                rest = [
                    (own_leaves + axis - 1) * groups + group for axis in (1, 2)
                ]
                gy = left[1] - q_rows[rest[0] : rest[0] + 1, :]
                gz = left[2] - q_rows[rest[1] : rest[1] + 1, :]
                dist = gx * gx + gy * gy + gz * gz
                k_buf[sub * SUB : (sub + 1) * SUB, group * LANES : (group + 1) * LANES] = jnp.exp(
                    -dist * spread
                ).astype(jnp.bfloat16)
        near_buf[tile] = jnp.dot(
            k_buf[...], x_buf[...], preferred_element_type=jnp.float32
        ) * (LEAF ** -0.5)
        copy = pltpu.make_async_copy(
            near_buf.at[tile], near_hbm.at[pl.ds(tile * TILE, TILE)], near_sem.at[tile]
        )
        copy.start()
        near_copies.append(copy)

    work = [functools.partial(near_tile, tile) for tile in range(own_rows // TILE)]
    stages = [reduce_blk] + [functools.partial(level, bit) for bit in range(levels)] + [mix]
    x_copy.wait()
    share = max(1, len(work) // (len(stages)))
    for stage in stages[:-1]:
        for _ in range(share):
            if work:
                work.pop(0)()
        for chunk in range(chunks):
            stage(chunk)
    for chunk in range(chunks):
        mix(chunk)
    while work:
        work.pop(0)()
    for chunk in range(chunks):
        for back in range(1, blk_count):
            pass_on(back, chunk)
    for copy in rep_copies.values():
        copy.wait_recv()
    mixed_out[...] = gather_buf[...].astype(jnp.bfloat16)
    for group in (blk_copies, pts_copies, all_copies, rep_copies):
        for copy in group.values():
            copy.wait_send()
    for copy in near_copies:
        copy.wait()


def finish_kernel(mixed, near_hbm, panels_hbm, out_hbm, p_buf, buf, p_sem, in_sem, out_sem):
    tiles = buf.shape[0]
    own_rows = tiles * TILE
    rep = lax.axis_index("rep")
    p_copy = pltpu.make_async_copy(
        panels_hbm.at[pl.ds(pl.multiple_of(rep * own_rows, TILE), own_rows)], p_buf, p_sem
    )
    p_copy.start()
    loads = []
    for tile in range(tiles):
        at = pl.ds(tile * TILE, TILE)
        loads.append(pltpu.make_async_copy(near_hbm.at[at], buf.at[tile], in_sem.at[tile]))
        loads[-1].start()
    p_copy.wait()
    stores = []
    for tile in range(tiles):
        at = pl.ds(tile * TILE, TILE)
        far = nt_dot(p_buf[at, :], mixed[...])
        loads[tile].wait()
        buf[tile] = buf[tile] + far
        stores.append(pltpu.make_async_copy(buf.at[tile], out_hbm.at[at], out_sem.at[tile]))
        stores[-1].start()
    for store in stores:
        store.wait()


def on_device(points_x, coords, panels, coupling, near_list, order):
    rows, nrhs = points_x.shape
    rank = panels.shape[1]
    blk_count = lax.axis_size("blk")
    rep_count = lax.axis_size("rep")
    levels = min(lax.axis_size("pts").bit_length() - 1, 4)
    half = nrhs // rep_count
    piece = half // blk_count
    own_rows = rows // rep_count
    tiles = own_rows // TILE
    groups = rows // LANES
    own_leaves = own_rows // LEAF
    chunks = 2
    vmem = pl.BlockSpec(memory_space=pltpu.VMEM)
    smem = pl.BlockSpec(memory_space=pltpu.SMEM)
    any_space = pl.BlockSpec(memory_space=pl.ANY)
    dma = pltpu.SemaphoreType.DMA
    f32 = jnp.float32

    coef, p_cols, q_rows = pl.pallas_call(
        prepare_kernel,
        out_shape=(
            jax.ShapeDtypeStruct((half, rank), f32),
            jax.ShapeDtypeStruct((own_rows, 8), f32),
            jax.ShapeDtypeStruct(((own_leaves + 2) * groups, LANES), f32),
        ),
        in_specs=[vmem, vmem, vmem, smem, vmem, vmem],
        out_specs=(vmem, vmem, vmem),
        compiler_params=pltpu.CompilerParams(vmem_limit_bytes=48 * 2**20),
        name="prepare",
    )(order.reshape(1, rows), order.reshape(groups, LANES), coords, near_list, panels, points_x)

    near, mixed = pl.pallas_call(
        functools.partial(exchange_kernel, levels, chunks),
        out_shape=(
            jax.ShapeDtypeStruct((own_rows, nrhs), f32),
            jax.ShapeDtypeStruct((nrhs, rank), jnp.bfloat16),
        ),
        in_specs=[vmem, vmem, vmem, vmem, any_space],
        out_specs=(any_space, vmem),
        scratch_shapes=[
            pltpu.VMEM((rows, nrhs), jnp.bfloat16),
            pltpu.VMEM((TILE, rows), jnp.bfloat16),
            pltpu.VMEM((tiles, TILE, nrhs), f32),
            pltpu.VMEM((blk_count - 1, piece, rank), f32),
            pltpu.VMEM((levels, piece, rank), f32),
            pltpu.VMEM((levels, piece, rank), f32),
            pltpu.VMEM((piece, rank), f32),
            pltpu.VMEM((nrhs, rank), f32),
            dma,
            dma((tiles,)),
            dma((blk_count - 1, chunks)),
            dma((blk_count - 1, chunks)),
            dma((levels, chunks)),
            dma((levels, chunks)),
            dma((blk_count - 1, chunks)),
            dma((blk_count - 1, chunks)),
            dma((rep_count - 1, blk_count, chunks)),
            dma((rep_count - 1, blk_count, chunks)),
        ],
        compiler_params=pltpu.CompilerParams(
            collective_id=0, has_side_effects=True, vmem_limit_bytes=48 * 2**20
        ),
        name="exchange",
    )(coef, coupling, p_cols, q_rows, points_x)

    return pl.pallas_call(
        finish_kernel,
        out_shape=jax.ShapeDtypeStruct((own_rows, nrhs), f32),
        in_specs=[vmem, any_space, any_space],
        out_specs=any_space,
        scratch_shapes=[
            pltpu.VMEM((own_rows, rank), jnp.bfloat16),
            pltpu.VMEM((tiles, TILE, nrhs), f32),
            dma,
            dma((tiles,)),
            dma((tiles,)),
        ],
        compiler_params=pltpu.CompilerParams(vmem_limit_bytes=48 * 2**20),
        name="finish",
    )(mixed, near, panels)


def solution(mesh):
    placed = (
        P(("groups", "pts", "blk"), None),
        P(None, ("groups", "pts", "blk")),
        P(("groups", "pts", "blk"), None),
        P(("groups", "pts"), None),
        P(("groups", "pts", "blk"), None),
        P(("groups", "pts", "blk")),
    )
    return jax.shard_map(
        on_device,
        mesh=mesh,
        in_specs=placed,
        out_specs=P(("groups", "pts", "blk", "rep"), None),
        check_vma=False,
    )
```

```python
import functools

import jax
import jax.numpy as jnp
from jax import lax
from jax.experimental import pallas as pl
from jax.experimental.pallas import tpu as pltpu
from jax.sharding import PartitionSpec as P

LEAF = 512
LANES = 128
TILE = 256
SUB = 64
FAR_AWAY = 1e18
CHUNKS = 2
NEAR_WAVES = (0, 0, 2, 4)
VMEM_MIB = 44
MESH = pl.DeviceIdType.MESH

spread = 1.0 / (2.0 * 0.1 * 0.1)


def nt_dot(left, right):
    return lax.dot_general(
        left, right, (((1,), (1,)), ((), ())), preferred_element_type=jnp.float32
    )


def tn_dot(left, right):
    return lax.dot_general(
        left, right, (((0,), (0,)), ((), ())), preferred_element_type=jnp.float32
    )


def exchange_kernel(
    levels,
    chunks,
    near_waves,
    order_row_hbm,
    order_tile_hbm,
    coords_hbm,
    list_hbm,
    panels_hbm,
    coupling_hbm,
    x_hbm,
    near_out,
    mixed_out,
    order_row,
    order_tile,
    coords,
    near_list,
    panels,
    coupling,
    x_buf,
    p_cols,
    q_rows,
    coef,
    k_buf,
    near_buf,
    part_buf,
    run_buf,
    pts_buf,
    inc_buf,
    all_buf,
    gather_buf,
    load_sem,
    near_sem,
    part_send,
    part_recv,
    pts_send,
    pts_recv,
    all_send,
    all_recv,
    rep_send,
    rep_recv,
):
    blk_count = lax.axis_size("blk")
    rep_count = lax.axis_size("rep")
    rep = lax.axis_index("rep")
    blk = lax.axis_index("blk")
    seg = lax.axis_index("pts")
    rows, nrhs = x_buf.shape
    start = (seg * blk_count + blk) * rows
    base_leaf = start // LEAF
    half = nrhs // rep_count
    piece = half // (2 * blk_count)
    step = piece // chunks
    groups = rows // LANES
    own_rows = rows // rep_count
    leaf_count = rows // LEAF
    own_leaves = own_rows // LEAF

    loads = []
    for source, target in (
        (order_row_hbm, order_row),
        (panels_hbm, panels),
        (x_hbm, x_buf),
        (order_tile_hbm, order_tile),
        (coords_hbm, coords),
        (list_hbm, near_list),
        (coupling_hbm, coupling),
    ):
        loads.append(pltpu.make_async_copy(source, target, load_sem.at[len(loads)]))
        loads[-1].start()

    def blk_peer(d):
        return lax.rem(blk + d, blk_count)

    def rep_peer(d):
        return lax.rem(rep + d, rep_count)

    def pts_peer(bit):
        mask = 2**bit
        return seg + mask - 2 * mask * lax.rem(lax.div(seg, mask), 2)

    offsets = [(other, d) for other in range(2) for d in range(blk_count)]

    def block_peer(other, d):
        return {"pts": pts_peer(0) if other else seg, "blk": blk_peer(d)}

    def slice_of(other, d):
        side = lax.rem(seg, 2)
        return ((1 - side if other else side) * blk_count + blk_peer(d)) * piece

    peers = [block_peer(*offset) for offset in offsets[1:]]
    peers += [{"rep": rep_peer(d)} for d in range(1, rep_count)]
    peers += [{"pts": pts_peer(bit)} for bit in range(1, levels)]
    barrier = pltpu.get_barrier_semaphore()
    for peer in peers:
        pl.semaphore_signal(barrier, inc=1, device_id=peer, device_id_type=MESH)

    loads[0].wait()
    local = order_row[...] - start
    high = lax.shift_right_logical(local, 8)
    low = (local & (TILE - 1)).astype(jnp.float32)
    columns = pl.ds(pl.multiple_of(rep * half, LANES), half)
    lane_at = (
        lax.broadcasted_iota(jnp.int32, (TILE, rows), 0).astype(jnp.float32).astype(jnp.bfloat16)
    )
    total = jnp.zeros(coef.shape, jnp.float32)
    for tile in range(rows // TILE):
        want = jnp.where(high == tile, low, -1.0).astype(jnp.bfloat16)
        chosen = jnp.where(lane_at == want, jnp.bfloat16(1), jnp.bfloat16(0))
        if tile == 0:
            loads[1].wait()
        moved = jnp.dot(chosen, panels[...], preferred_element_type=jnp.float32)
        if tile == 0:
            loads[2].wait()
        total = total + tn_dot(
            x_buf[pl.ds(tile * TILE, TILE), columns], moved.astype(jnp.bfloat16)
        )
    coef[...] = total

    pl.semaphore_wait(barrier, len(peers))

    def remote(src, dst, send, recv, peer):
        return pltpu.make_async_remote_copy(
            src_ref=src, dst_ref=dst, send_sem=send, recv_sem=recv,
            device_id=peer, device_id_type=MESH,
        )

    def rows_of(first, chunk):
        return pl.ds(pl.multiple_of(first + chunk * step, 8), step)

    def at_of(chunk):
        return pl.ds(chunk * step, step)

    def part_copy(at, chunk):
        return remote(
            coef.at[rows_of(slice_of(*offsets[at]), chunk)],
            part_buf.at[at, at_of(chunk)],
            part_send.at[at, chunk],
            part_recv.at[at, chunk],
            block_peer(*offsets[at]),
        )

    def level_copy(bit, chunk):
        return remote(
            run_buf.at[bit - 1, at_of(chunk)],
            pts_buf.at[bit - 1, at_of(chunk)],
            pts_send.at[bit - 1, chunk],
            pts_recv.at[bit - 1, chunk],
            {"pts": pts_peer(bit)},
        )

    def all_copy(at, chunk):
        return remote(
            inc_buf.at[offsets[at][0], at_of(chunk)],
            all_buf.at[at, at_of(chunk)],
            all_send.at[at, chunk],
            all_recv.at[at, chunk],
            block_peer(*offsets[at]),
        )

    def source_rows(at, chunk):
        other, d = offsets[at]
        return rows_of(rep * half + slice_of(other, blk_count - d), chunk)

    def rep_copy(d, at, chunk):
        rows_at = source_rows(at, chunk)
        return remote(
            gather_buf.at[rows_at], gather_buf.at[rows_at],
            rep_send.at[d - 1, at, chunk], rep_recv.at[d - 1, at, chunk],
            {"rep": rep_peer(d)},
        )

    for chunk in range(chunks):
        for at in range(1, len(offsets)):
            part_copy(at, chunk).start()

    def reduce_parts(chunk):
        at = at_of(chunk)
        sums = [coef[rows_of(slice_of(0, 0), chunk), :], None]
        for index in range(1, len(offsets)):
            part_copy(index, chunk).wait_recv()
            got = part_buf[index, at, :]
            other = offsets[index][0]
            sums[other] = got if sums[other] is None else sums[other] + got
        run_buf[0, at, :] = sums[0] + sums[1]
        if levels > 1:
            level_copy(1, chunk).start()
        inc_buf[0, at, :] = sums[1]
        inc_buf[1, at, :] = sums[0]
        if levels == 1:
            share(chunk)

    def level(bit, chunk):
        at = at_of(chunk)
        level_copy(bit, chunk).wait_recv()
        got = pts_buf[bit - 1, at, :]
        if bit + 1 < levels:
            run_buf[bit, at, :] = run_buf[bit - 1, at, :] + got
            level_copy(bit + 1, chunk).start()
        scaled = 2.0 ** (-0.5 * bit) * got
        for other in range(2):
            inc_buf[other, at, :] = inc_buf[other, at, :] + scaled
        if bit + 1 == levels:
            share(chunk)

    def mix(at, chunk, value):
        top = value.astype(jnp.bfloat16)
        rest = value - top.astype(jnp.float32)
        middle = rest.astype(jnp.bfloat16)
        bottom = (rest - middle.astype(jnp.float32)).astype(jnp.bfloat16)
        mats = coupling[...]
        mixed = nt_dot(bottom, mats) + nt_dot(middle, mats) + nt_dot(top, mats)
        gather_buf[source_rows(at, chunk), :] = mixed.astype(jnp.bfloat16).astype(jnp.float32)
        for d in range(1, rep_count):
            rep_copy(d, at, chunk).start()

    def share(chunk):
        for index in range(1, len(offsets)):
            all_copy(index, chunk).start()
        mix(0, chunk, inc_buf[0, at_of(chunk), :])

    def pass_on(chunk):
        for index in range(1, len(offsets)):
            all_copy(index, chunk).wait_recv()
            mix(index, chunk, all_buf[index, at_of(chunk), :])

    for load in loads[3:]:
        load.wait()
    per_core = own_rows // LANES
    own = order_tile[pl.ds(pl.multiple_of(rep * per_core, 8), per_core), :] - start
    own_high = lax.shift_right_logical(own, 7)
    own_low = own & (LANES - 1)
    picked = []
    for axis in range(3):
        value = jnp.zeros((per_core, LANES), jnp.float32)
        for group in range(groups):
            source = jnp.broadcast_to(
                coords[axis : axis + 1, group * LANES : (group + 1) * LANES], (per_core, LANES)
            )
            got = jnp.take_along_axis(source, own_low, axis=1, mode="promise_in_bounds")
            value = jnp.where(own_high == group, got, value)
        picked.append(value)
    blank = jnp.zeros((5, LANES), jnp.float32)
    pieces = []
    for row in range(per_core):
        pieces += [value[row : row + 1] for value in picked] + [blank]
    pieces.append(jnp.zeros((LANES - 8 * per_core, LANES), jnp.float32))
    turned = jnp.concatenate(pieces, axis=0).T
    for row in range(per_core):
        p_cols[row * LANES : (row + 1) * LANES, :] = turned[:, row * 8 : (row + 1) * 8]

    high7 = lax.shift_right_logical(local, 7)
    low7 = local & (LANES - 1)
    leaf_at = lax.broadcasted_iota(jnp.int32, (1, rows), 1) // LEAF
    key = leaf_at * groups + high7
    left = lax.broadcasted_iota(jnp.int32, (leaf_count * groups, rows), 0) == key
    right = lax.broadcasted_iota(jnp.int32, (LANES, rows), 0) == low7
    member = nt_dot(
        jnp.where(left, 1.0, 0.0).astype(jnp.bfloat16),
        jnp.where(right, 1.0, 0.0).astype(jnp.bfloat16),
    )
    folded = [
        jnp.concatenate(
            [coords[axis : axis + 1, g * LANES : (g + 1) * LANES] for g in range(groups)], axis=0
        )
        for axis in range(3)
    ]
    for own_leaf in range(own_leaves):
        entries = near_list[pl.ds(rep * own_leaves + own_leaf, 1), :] - base_leaf
        live = jnp.zeros((groups, LANES), jnp.float32)
        for other in range(leaf_count):
            hit = jnp.where(entries == other, 1.0, 0.0)
            weight = jnp.sum(hit, axis=1, keepdims=True)
            live = live + weight * member[other * groups : (other + 1) * groups]
        q_rows[own_leaf * groups : (own_leaf + 1) * groups, :] = jnp.where(
            live > 0.5, folded[0], FAR_AWAY
        )
    for axis in (1, 2):
        at = (own_leaves + axis - 1) * groups
        q_rows[at : at + groups, :] = folded[axis]

    def near_tile(tile):
        leaf = tile * TILE // LEAF
        for sub in range(TILE // SUB):
            at = tile * TILE + sub * SUB
            left = [
                jnp.broadcast_to(p_cols[at : at + SUB, axis : axis + 1], (SUB, LANES))
                for axis in range(3)
            ]
            for group in range(groups):
                gap = []
                for axis in range(3):
                    row = (leaf if axis == 0 else own_leaves + axis - 1) * groups + group
                    gap.append(left[axis] - q_rows[row : row + 1, :])
                dist = gap[0] * gap[0] + gap[1] * gap[1] + gap[2] * gap[2]
                k_buf[sub * SUB : (sub + 1) * SUB, group * LANES : (group + 1) * LANES] = jnp.exp(
                    -dist * spread
                ).astype(jnp.bfloat16)
        near_buf[tile] = jnp.dot(
            k_buf[...], x_buf[...], preferred_element_type=jnp.float32
        ) * (LEAF ** -0.5)
        near_copy(tile).start()

    def near_copy(tile):
        return pltpu.make_async_copy(
            near_buf.at[tile], near_out.at[pl.ds(tile * TILE, TILE)], near_sem.at[tile]
        )

    stages = [reduce_parts]
    stages += [functools.partial(level, bit) for bit in range(1, levels)]
    stages.append(pass_on)
    lag = chunks
    tile_at = 0
    for wave in range(chunks + lag * (len(stages) - 1)):
        for _ in range(near_waves.count(wave)):
            if tile_at < own_rows // TILE:
                near_tile(tile_at)
                tile_at += 1
        for at, stage in enumerate(stages):
            chunk = wave - lag * at
            if 0 <= chunk < chunks:
                stage(chunk)
    for tile in range(tile_at, own_rows // TILE):
        near_tile(tile)
    for chunk in range(chunks):
        for at in range(len(offsets)):
            for d in range(1, rep_count):
                rep_copy(d, at, chunk).wait_recv()
    mixed_out[...] = gather_buf[...].astype(jnp.bfloat16)
    for chunk in range(chunks):
        for at in range(len(offsets)):
            if at:
                part_copy(at, chunk).wait_send()
                all_copy(at, chunk).wait_send()
            for d in range(1, rep_count):
                rep_copy(d, at, chunk).wait_send()
        for bit in range(1, levels):
            level_copy(bit, chunk).wait_send()
    for tile in range(own_rows // TILE):
        near_copy(tile).wait()


def finish_kernel(mixed, near, panels, out_hbm, buf, out_sem):
    tiles = buf.shape[0]
    rep = lax.axis_index("rep")
    stores = []
    for tile in range(tiles):
        at = pl.ds(tile * TILE, TILE)
        own = pl.ds(pl.multiple_of((rep * tiles + tile) * TILE, TILE), TILE)
        buf[tile] = near[at, :] + nt_dot(panels[own, :], mixed[...])
        stores.append(pltpu.make_async_copy(buf.at[tile], out_hbm.at[at], out_sem.at[tile]))
        stores[-1].start()
    for store in stores:
        store.wait()


def on_device(points_x, coords, panels, coupling, near_list, order):
    rows, nrhs = points_x.shape
    rank = panels.shape[1]
    blk_count = lax.axis_size("blk")
    rep_count = lax.axis_size("rep")
    levels = min(lax.axis_size("pts").bit_length() - 1, 4)
    half = nrhs // rep_count
    piece = half // (2 * blk_count)
    own_rows = rows // rep_count
    tiles = own_rows // TILE
    groups = rows // LANES
    own_leaves = own_rows // LEAF
    chunks = CHUNKS
    slots = max(levels - 1, 1)
    members = 2 * blk_count
    vmem = pl.BlockSpec(memory_space=pltpu.VMEM)
    any_space = pl.BlockSpec(memory_space=pl.ANY)
    dma = pltpu.SemaphoreType.DMA
    f32 = jnp.float32
    bf16 = jnp.bfloat16

    operands = (
        order.reshape(1, rows), order.reshape(groups, LANES), coords, near_list, panels, coupling, points_x
    )
    near, mixed = pl.pallas_call(
        functools.partial(exchange_kernel, levels, chunks, NEAR_WAVES),
        out_shape=(
            jax.ShapeDtypeStruct((own_rows, nrhs), f32),
            jax.ShapeDtypeStruct((nrhs, rank), bf16),
        ),
        in_specs=[pl.BlockSpec(memory_space=pltpu.HBM)] * 7,
        out_specs=(any_space, vmem),
        scratch_shapes=[
            pltpu.VMEM((1, rows), jnp.int32),
            pltpu.VMEM((groups, LANES), jnp.int32),
            pltpu.VMEM((3, rows), f32),
            pltpu.VMEM(near_list.shape, jnp.int32),
            pltpu.VMEM((rows, rank), bf16),
            pltpu.VMEM((rank, rank), bf16),
            pltpu.VMEM((rows, nrhs), bf16),
            pltpu.VMEM((own_rows, 8), f32),
            pltpu.VMEM(((own_leaves + 2) * groups, LANES), f32),
            pltpu.VMEM((half, rank), f32),
            pltpu.VMEM((TILE, rows), bf16),
            pltpu.VMEM((tiles, TILE, nrhs), f32),
            pltpu.VMEM((members, piece, rank), f32),
            pltpu.VMEM((slots, piece, rank), f32),
            pltpu.VMEM((slots, piece, rank), f32),
            pltpu.VMEM((2, piece, rank), f32),
            pltpu.VMEM((members, piece, rank), f32),
            pltpu.VMEM((nrhs, rank), f32),
            dma((7,)),
            dma((tiles,)),
            dma((members, chunks)),
            dma((members, chunks)),
            dma((slots, chunks)),
            dma((slots, chunks)),
            dma((members, chunks)),
            dma((members, chunks)),
            dma((rep_count - 1, members, chunks)),
            dma((rep_count - 1, members, chunks)),
        ],
        compiler_params=pltpu.CompilerParams(
            collective_id=0, has_side_effects=True, vmem_limit_bytes=VMEM_MIB * 2**20
        ),
        name="exchange",
    )(*[pltpu.with_memory_space_constraint(value, pltpu.HBM) for value in operands])

    return pl.pallas_call(
        finish_kernel,
        out_shape=jax.ShapeDtypeStruct((own_rows, nrhs), f32),
        in_specs=[vmem, vmem, vmem],
        out_specs=any_space,
        scratch_shapes=[
            pltpu.VMEM((tiles, TILE, nrhs), f32),
            dma((tiles,)),
        ],
        compiler_params=pltpu.CompilerParams(vmem_limit_bytes=32 * 2**20),
        name="finish",
    )(mixed, near, panels)


def solution(mesh):
    placed = (
        P(("groups", "pts", "blk"), None),
        P(None, ("groups", "pts", "blk")),
        P(("groups", "pts", "blk"), None),
        P(("groups", "pts"), None),
        P(("groups", "pts", "blk"), None),
        P(("groups", "pts", "blk")),
    )
    return jax.shard_map(
        on_device,
        mesh=mesh,
        in_specs=placed,
        out_specs=P(("groups", "pts", "blk", "rep"), None),
        check_vma=False,
    )
```

```python
import functools

import jax
import jax.numpy as jnp
from jax import lax
from jax.experimental import pallas as pl
from jax.experimental.pallas import tpu as pltpu
from jax.sharding import PartitionSpec as P

LEAF = 512
LANES = 128
TILE = 256
SUB = 64
FAR_AWAY = 1e18
CHUNKS = 2
NEAR_WAVES = (0, 0, 2, 4)
VMEM_MIB = 44
MESH = pl.DeviceIdType.MESH

spread = 1.0 / (2.0 * 0.1 * 0.1)


def nt_dot(left, right):
    return lax.dot_general(
        left, right, (((1,), (1,)), ((), ())), preferred_element_type=jnp.float32
    )


def tn_dot(left, right):
    return lax.dot_general(
        left, right, (((0,), (0,)), ((), ())), preferred_element_type=jnp.float32
    )


def exchange_kernel(
    levels,
    chunks,
    near_waves,
    order_row_hbm,
    order_tile_hbm,
    coords_hbm,
    list_hbm,
    panels_hbm,
    coupling_hbm,
    x_hbm,
    near_out,
    mixed_out,
    order_row,
    order_tile,
    coords,
    near_list,
    panels,
    coupling,
    x_buf,
    p_cols,
    q_rows,
    coef,
    k_buf,
    near_buf,
    part_buf,
    run_buf,
    pts_buf,
    inc_buf,
    all_buf,
    gather_buf,
    load_sem,
    near_sem,
    part_send,
    part_recv,
    pts_send,
    pts_recv,
    all_send,
    all_recv,
    rep_send,
    rep_recv,
):
    blk_count = lax.axis_size("blk")
    rep_count = lax.axis_size("rep")
    rep = lax.axis_index("rep")
    blk = lax.axis_index("blk")
    seg = lax.axis_index("pts")
    rows, nrhs = x_buf.shape
    start = (seg * blk_count + blk) * rows
    base_leaf = start // LEAF
    half = nrhs // rep_count
    piece = half // (2 * blk_count)
    step = piece // chunks
    groups = rows // LANES
    own_rows = rows // rep_count
    leaf_count = rows // LEAF
    own_leaves = own_rows // LEAF

    loads = []
    for source, target in (
        (order_row_hbm, order_row),
        (panels_hbm, panels),
        (x_hbm, x_buf),
        (order_tile_hbm, order_tile),
        (coords_hbm, coords),
        (list_hbm, near_list),
        (coupling_hbm, coupling),
    ):
        loads.append(pltpu.make_async_copy(source, target, load_sem.at[len(loads)]))
        loads[-1].start()

    def blk_peer(d):
        return lax.rem(blk + d, blk_count)

    def rep_peer(d):
        return lax.rem(rep + d, rep_count)

    def pts_peer(bit):
        mask = 2**bit
        return seg + mask - 2 * mask * lax.rem(lax.div(seg, mask), 2)

    offsets = [(other, d) for other in range(2) for d in range(blk_count)]

    def block_peer(other, d):
        return {"pts": pts_peer(0) if other else seg, "blk": blk_peer(d)}

    def slice_of(other, d):
        side = lax.rem(seg, 2)
        return ((1 - side if other else side) * blk_count + blk_peer(d)) * piece

    peers = [block_peer(*offset) for offset in offsets[1:]]
    peers += [{"rep": rep_peer(d)} for d in range(1, rep_count)]
    peers += [{"pts": pts_peer(bit)} for bit in range(1, levels)]
    barrier = pltpu.get_barrier_semaphore()
    for peer in peers:
        pl.semaphore_signal(barrier, inc=1, device_id=peer, device_id_type=MESH)

    loads[0].wait()
    local = order_row[...] - start
    high = lax.shift_right_logical(local, 8)
    low = (local & (TILE - 1)).astype(jnp.float32)
    columns = pl.ds(pl.multiple_of(rep * half, LANES), half)
    lane_at = (
        lax.broadcasted_iota(jnp.int32, (TILE, rows), 0).astype(jnp.float32).astype(jnp.bfloat16)
    )
    lows = jnp.where(lane_at == low.astype(jnp.bfloat16), jnp.bfloat16(1), jnp.bfloat16(0))
    moved = []
    for tile in range(rows // TILE):
        chosen = lows * jnp.where(high == tile, 1.0, 0.0).astype(jnp.bfloat16)
        if tile == 0:
            loads[1].wait()
        moved.append(
            jnp.dot(chosen, panels[...], preferred_element_type=jnp.float32).astype(jnp.bfloat16)
        )
    loads[2].wait()
    total = tn_dot(x_buf[:, columns], jnp.concatenate(moved, axis=0))
    coef[...] = total

    pl.semaphore_wait(barrier, len(peers))

    def remote(src, dst, send, recv, peer):
        return pltpu.make_async_remote_copy(
            src_ref=src, dst_ref=dst, send_sem=send, recv_sem=recv,
            device_id=peer, device_id_type=MESH,
        )

    def rows_of(first, chunk):
        return pl.ds(pl.multiple_of(first + chunk * step, 8), step)

    def at_of(chunk):
        return pl.ds(chunk * step, step)

    def part_copy(at, chunk):
        return remote(
            coef.at[rows_of(slice_of(*offsets[at]), chunk)],
            part_buf.at[at, at_of(chunk)],
            part_send.at[at, chunk],
            part_recv.at[at, chunk],
            block_peer(*offsets[at]),
        )

    def level_copy(bit, chunk):
        return remote(
            run_buf.at[bit - 1, at_of(chunk)],
            pts_buf.at[bit - 1, at_of(chunk)],
            pts_send.at[bit - 1, chunk],
            pts_recv.at[bit - 1, chunk],
            {"pts": pts_peer(bit)},
        )

    def all_copy(at, chunk):
        return remote(
            inc_buf.at[offsets[at][0], at_of(chunk)],
            all_buf.at[at, at_of(chunk)],
            all_send.at[at, chunk],
            all_recv.at[at, chunk],
            block_peer(*offsets[at]),
        )

    def source_rows(at, chunk):
        other, d = offsets[at]
        return rows_of(rep * half + slice_of(other, blk_count - d), chunk)

    def rep_copy(d, at, chunk):
        rows_at = source_rows(at, chunk)
        return remote(
            gather_buf.at[rows_at], gather_buf.at[rows_at],
            rep_send.at[d - 1, at, chunk], rep_recv.at[d - 1, at, chunk],
            {"rep": rep_peer(d)},
        )

    for chunk in range(chunks):
        for at in range(1, len(offsets)):
            part_copy(at, chunk).start()

    def reduce_parts(chunk):
        at = at_of(chunk)
        sums = [coef[rows_of(slice_of(0, 0), chunk), :], None]
        for index in range(1, len(offsets)):
            part_copy(index, chunk).wait_recv()
            got = part_buf[index, at, :]
            other = offsets[index][0]
            sums[other] = got if sums[other] is None else sums[other] + got
        run_buf[0, at, :] = sums[0] + sums[1]
        if levels > 1:
            level_copy(1, chunk).start()
        inc_buf[0, at, :] = sums[1]
        inc_buf[1, at, :] = sums[0]
        if levels == 1:
            share(chunk)

    def level(bit, chunk):
        at = at_of(chunk)
        level_copy(bit, chunk).wait_recv()
        got = pts_buf[bit - 1, at, :]
        if bit + 1 < levels:
            run_buf[bit, at, :] = run_buf[bit - 1, at, :] + got
            level_copy(bit + 1, chunk).start()
        scaled = 2.0 ** (-0.5 * bit) * got
        for other in range(2):
            inc_buf[other, at, :] = inc_buf[other, at, :] + scaled
        if bit + 1 == levels:
            share(chunk)

    def mix(at, chunk, value):
        top = value.astype(jnp.bfloat16)
        rest = value - top.astype(jnp.float32)
        middle = rest.astype(jnp.bfloat16)
        bottom = (rest - middle.astype(jnp.float32)).astype(jnp.bfloat16)
        mats = coupling[...]
        mixed = nt_dot(bottom, mats) + nt_dot(middle, mats) + nt_dot(top, mats)
        gather_buf[source_rows(at, chunk), :] = mixed.astype(jnp.bfloat16).astype(jnp.float32)
        for d in range(1, rep_count):
            rep_copy(d, at, chunk).start()

    def share(chunk):
        for index in range(1, len(offsets)):
            all_copy(index, chunk).start()
        mix(0, chunk, inc_buf[0, at_of(chunk), :])

    def pass_on(chunk):
        for index in range(1, len(offsets)):
            all_copy(index, chunk).wait_recv()
            mix(index, chunk, all_buf[index, at_of(chunk), :])

    for load in loads[3:]:
        load.wait()
    per_core = own_rows // LANES
    own = order_tile[pl.ds(pl.multiple_of(rep * per_core, 8), per_core), :] - start
    own_high = lax.shift_right_logical(own, 7)
    own_low = own & (LANES - 1)
    picked = []
    for axis in range(3):
        value = jnp.zeros((per_core, LANES), jnp.float32)
        for group in range(groups):
            source = jnp.broadcast_to(
                coords[axis : axis + 1, group * LANES : (group + 1) * LANES], (per_core, LANES)
            )
            got = jnp.take_along_axis(source, own_low, axis=1, mode="promise_in_bounds")
            value = jnp.where(own_high == group, got, value)
        picked.append(value)
    blank = jnp.zeros((5, LANES), jnp.float32)
    pieces = []
    for row in range(per_core):
        pieces += [value[row : row + 1] for value in picked] + [blank]
    pieces.append(jnp.zeros((LANES - 8 * per_core, LANES), jnp.float32))
    turned = jnp.concatenate(pieces, axis=0).T
    for row in range(per_core):
        p_cols[row * LANES : (row + 1) * LANES, :] = turned[:, row * 8 : (row + 1) * 8]

    high7 = lax.shift_right_logical(local, 7)
    low7 = local & (LANES - 1)
    leaf_at = lax.broadcasted_iota(jnp.int32, (1, rows), 1) // LEAF
    key = leaf_at * groups + high7
    left = lax.broadcasted_iota(jnp.int32, (leaf_count * groups, rows), 0) == key
    right = lax.broadcasted_iota(jnp.int32, (LANES, rows), 0) == low7
    member = nt_dot(
        jnp.where(left, 1.0, 0.0).astype(jnp.bfloat16),
        jnp.where(right, 1.0, 0.0).astype(jnp.bfloat16),
    )
    folded = [
        jnp.concatenate(
            [coords[axis : axis + 1, g * LANES : (g + 1) * LANES] for g in range(groups)], axis=0
        )
        for axis in range(3)
    ]
    for own_leaf in range(own_leaves):
        entries = near_list[pl.ds(rep * own_leaves + own_leaf, 1), :] - base_leaf
        live = jnp.zeros((groups, LANES), jnp.float32)
        for other in range(leaf_count):
            hit = jnp.where(entries == other, 1.0, 0.0)
            weight = jnp.sum(hit, axis=1, keepdims=True)
            live = live + weight * member[other * groups : (other + 1) * groups]
        q_rows[own_leaf * groups : (own_leaf + 1) * groups, :] = jnp.where(
            live > 0.5, folded[0], FAR_AWAY
        )
    for axis in (1, 2):
        at = (own_leaves + axis - 1) * groups
        q_rows[at : at + groups, :] = folded[axis]

    def near_tile(tile):
        leaf = tile * TILE // LEAF
        for sub in range(TILE // SUB):
            at = tile * TILE + sub * SUB
            left = [
                jnp.broadcast_to(p_cols[at : at + SUB, axis : axis + 1], (SUB, LANES))
                for axis in range(3)
            ]
            for group in range(groups):
                gap = []
                for axis in range(3):
                    row = (leaf if axis == 0 else own_leaves + axis - 1) * groups + group
                    gap.append(left[axis] - q_rows[row : row + 1, :])
                dist = gap[0] * gap[0] + gap[1] * gap[1] + gap[2] * gap[2]
                k_buf[sub * SUB : (sub + 1) * SUB, group * LANES : (group + 1) * LANES] = jnp.exp(
                    -dist * spread
                ).astype(jnp.bfloat16)
        near_buf[tile] = jnp.dot(
            k_buf[...], x_buf[...], preferred_element_type=jnp.float32
        ) * (LEAF ** -0.5)
        near_copy(tile).start()

    def near_copy(tile):
        return pltpu.make_async_copy(
            near_buf.at[tile], near_out.at[pl.ds(tile * TILE, TILE)], near_sem.at[tile]
        )

    stages = [reduce_parts]
    stages += [functools.partial(level, bit) for bit in range(1, levels)]
    stages.append(pass_on)
    lag = chunks
    tile_at = 0
    for wave in range(chunks + lag * (len(stages) - 1)):
        for _ in range(near_waves.count(wave)):
            if tile_at < own_rows // TILE:
                near_tile(tile_at)
                tile_at += 1
        for at, stage in enumerate(stages):
            chunk = wave - lag * at
            if 0 <= chunk < chunks:
                stage(chunk)
    for tile in range(tile_at, own_rows // TILE):
        near_tile(tile)
    for chunk in range(chunks):
        for at in range(len(offsets)):
            for d in range(1, rep_count):
                rep_copy(d, at, chunk).wait_recv()
    mixed_out[...] = gather_buf[...].astype(jnp.bfloat16)
    for chunk in range(chunks):
        for at in range(len(offsets)):
            if at:
                part_copy(at, chunk).wait_send()
                all_copy(at, chunk).wait_send()
            for d in range(1, rep_count):
                rep_copy(d, at, chunk).wait_send()
        for bit in range(1, levels):
            level_copy(bit, chunk).wait_send()
    for tile in range(own_rows // TILE):
        near_copy(tile).wait()


def finish_kernel(mixed, near, panels, out_hbm, buf, out_sem):
    tiles = buf.shape[0]
    rep = lax.axis_index("rep")
    stores = []
    for tile in range(tiles):
        at = pl.ds(tile * TILE, TILE)
        own = pl.ds(pl.multiple_of((rep * tiles + tile) * TILE, TILE), TILE)
        buf[tile] = near[at, :] + nt_dot(panels[own, :], mixed[...])
        stores.append(pltpu.make_async_copy(buf.at[tile], out_hbm.at[at], out_sem.at[tile]))
        stores[-1].start()
    for store in stores:
        store.wait()


def on_device(points_x, coords, panels, coupling, near_list, order):
    rows, nrhs = points_x.shape
    rank = panels.shape[1]
    blk_count = lax.axis_size("blk")
    rep_count = lax.axis_size("rep")
    levels = min(lax.axis_size("pts").bit_length() - 1, 4)
    half = nrhs // rep_count
    piece = half // (2 * blk_count)
    own_rows = rows // rep_count
    tiles = own_rows // TILE
    groups = rows // LANES
    own_leaves = own_rows // LEAF
    chunks = CHUNKS
    slots = max(levels - 1, 1)
    members = 2 * blk_count
    vmem = pl.BlockSpec(memory_space=pltpu.VMEM)
    any_space = pl.BlockSpec(memory_space=pl.ANY)
    dma = pltpu.SemaphoreType.DMA
    f32 = jnp.float32
    bf16 = jnp.bfloat16

    operands = (
        order.reshape(1, rows), order.reshape(groups, LANES), coords, near_list, panels, coupling, points_x
    )
    near, mixed = pl.pallas_call(
        functools.partial(exchange_kernel, levels, chunks, NEAR_WAVES),
        out_shape=(
            jax.ShapeDtypeStruct((own_rows, nrhs), f32),
            jax.ShapeDtypeStruct((nrhs, rank), bf16),
        ),
        in_specs=[pl.BlockSpec(memory_space=pltpu.HBM)] * 7,
        out_specs=(any_space, vmem),
        scratch_shapes=[
            pltpu.VMEM((1, rows), jnp.int32),
            pltpu.VMEM((groups, LANES), jnp.int32),
            pltpu.VMEM((3, rows), f32),
            pltpu.VMEM(near_list.shape, jnp.int32),
            pltpu.VMEM((rows, rank), bf16),
            pltpu.VMEM((rank, rank), bf16),
            pltpu.VMEM((rows, nrhs), bf16),
            pltpu.VMEM((own_rows, 8), f32),
            pltpu.VMEM(((own_leaves + 2) * groups, LANES), f32),
            pltpu.VMEM((half, rank), f32),
            pltpu.VMEM((TILE, rows), bf16),
            pltpu.VMEM((tiles, TILE, nrhs), f32),
            pltpu.VMEM((members, piece, rank), f32),
            pltpu.VMEM((slots, piece, rank), f32),
            pltpu.VMEM((slots, piece, rank), f32),
            pltpu.VMEM((2, piece, rank), f32),
            pltpu.VMEM((members, piece, rank), f32),
            pltpu.VMEM((nrhs, rank), f32),
            dma((7,)),
            dma((tiles,)),
            dma((members, chunks)),
            dma((members, chunks)),
            dma((slots, chunks)),
            dma((slots, chunks)),
            dma((members, chunks)),
            dma((members, chunks)),
            dma((rep_count - 1, members, chunks)),
            dma((rep_count - 1, members, chunks)),
        ],
        compiler_params=pltpu.CompilerParams(
            collective_id=0, has_side_effects=True, vmem_limit_bytes=VMEM_MIB * 2**20
        ),
        name="exchange",
    )(*[pltpu.with_memory_space_constraint(value, pltpu.HBM) for value in operands])

    return pl.pallas_call(
        finish_kernel,
        out_shape=jax.ShapeDtypeStruct((own_rows, nrhs), f32),
        in_specs=[vmem, vmem, vmem],
        out_specs=any_space,
        scratch_shapes=[
            pltpu.VMEM((tiles, TILE, nrhs), f32),
            dma((tiles,)),
        ],
        compiler_params=pltpu.CompilerParams(vmem_limit_bytes=32 * 2**20),
        name="finish",
    )(mixed, near, panels)


def solution(mesh):
    placed = (
        P(("groups", "pts", "blk"), None),
        P(None, ("groups", "pts", "blk")),
        P(("groups", "pts", "blk"), None),
        P(("groups", "pts"), None),
        P(("groups", "pts", "blk"), None),
        P(("groups", "pts", "blk")),
    )
    return jax.shard_map(
        on_device,
        mesh=mesh,
        in_specs=placed,
        out_specs=P(("groups", "pts", "blk", "rep"), None),
        check_vma=False,
    )
```

```python
import functools

import jax
import jax.numpy as jnp
from jax import lax
from jax.experimental import pallas as pl
from jax.experimental.pallas import tpu as pltpu
from jax.sharding import PartitionSpec as P

LEAF = 512
LANES = 128
TILE = 256
SUB = 64
FAR_AWAY = 1e18
CHUNKS = 2
NEAR_WAVES = (0, 2, 2, 4)
VMEM_MIB = 44
MESH = pl.DeviceIdType.MESH

spread = 1.0 / (2.0 * 0.1 * 0.1)


def nt_dot(left, right):
    return lax.dot_general(
        left, right, (((1,), (1,)), ((), ())), preferred_element_type=jnp.float32
    )


def tn_dot(left, right):
    return lax.dot_general(
        left, right, (((0,), (0,)), ((), ())), preferred_element_type=jnp.float32
    )


def exchange_kernel(
    levels,
    chunks,
    near_waves,
    order_row_hbm,
    order_tile_hbm,
    coords_hbm,
    list_hbm,
    panels_hbm,
    coupling_hbm,
    x_hbm,
    near_out,
    mixed_out,
    order_row,
    order_tile,
    coords,
    near_list,
    panels,
    coupling,
    x_buf,
    p_cols,
    q_rows,
    coef,
    k_buf,
    near_buf,
    part_buf,
    run_buf,
    pts_buf,
    inc_buf,
    all_buf,
    gather_buf,
    load_sem,
    near_sem,
    part_send,
    part_recv,
    pts_send,
    pts_recv,
    all_send,
    all_recv,
    rep_send,
    rep_recv,
):
    blk_count = lax.axis_size("blk")
    rep_count = lax.axis_size("rep")
    rep = lax.axis_index("rep")
    blk = lax.axis_index("blk")
    seg = lax.axis_index("pts")
    rows, nrhs = x_buf.shape
    start = (seg * blk_count + blk) * rows
    base_leaf = start // LEAF
    half = nrhs // rep_count
    piece = half // (2 * blk_count)
    step = piece // chunks
    groups = rows // LANES
    own_rows = rows // rep_count
    leaf_count = rows // LEAF
    own_leaves = own_rows // LEAF

    loads = []
    for source, target in (
        (order_row_hbm, order_row),
        (panels_hbm, panels),
        (x_hbm, x_buf),
        (order_tile_hbm, order_tile),
        (coords_hbm, coords),
        (list_hbm, near_list),
        (coupling_hbm, coupling),
    ):
        loads.append(pltpu.make_async_copy(source, target, load_sem.at[len(loads)]))
        loads[-1].start()

    def blk_peer(d):
        return lax.rem(blk + d, blk_count)

    def rep_peer(d):
        return lax.rem(rep + d, rep_count)

    def pts_peer(bit):
        mask = 2**bit
        return seg + mask - 2 * mask * lax.rem(lax.div(seg, mask), 2)

    offsets = [(other, d) for other in range(2) for d in range(blk_count)]

    def block_peer(other, d):
        return {"pts": pts_peer(0) if other else seg, "blk": blk_peer(d)}

    def slice_of(other, d):
        side = lax.rem(seg, 2)
        return ((1 - side if other else side) * blk_count + blk_peer(d)) * piece

    peers = [block_peer(*offset) for offset in offsets[1:]]
    peers += [{"rep": rep_peer(d)} for d in range(1, rep_count)]
    peers += [{"pts": pts_peer(bit)} for bit in range(1, levels)]
    barrier = pltpu.get_barrier_semaphore()
    for peer in peers:
        pl.semaphore_signal(barrier, inc=1, device_id=peer, device_id_type=MESH)

    loads[0].wait()
    local = order_row[...] - start
    high = lax.shift_right_logical(local, 8)
    low = (local & (TILE - 1)).astype(jnp.float32)
    columns = pl.ds(pl.multiple_of(rep * half, LANES), half)
    lane_at = (
        lax.broadcasted_iota(jnp.int32, (TILE, rows), 0).astype(jnp.float32).astype(jnp.bfloat16)
    )
    lows = jnp.where(lane_at == low.astype(jnp.bfloat16), jnp.bfloat16(1), jnp.bfloat16(0))
    moved = []
    for tile in range(rows // TILE):
        chosen = lows * jnp.where(high == tile, 1.0, 0.0).astype(jnp.bfloat16)
        if tile == 0:
            loads[1].wait()
        moved.append(
            jnp.dot(chosen, panels[...], preferred_element_type=jnp.float32).astype(jnp.bfloat16)
        )
    loads[2].wait()
    total = tn_dot(x_buf[:, columns], jnp.concatenate(moved, axis=0))
    coef[...] = total

    pl.semaphore_wait(barrier, len(peers))

    def remote(src, dst, send, recv, peer):
        return pltpu.make_async_remote_copy(
            src_ref=src, dst_ref=dst, send_sem=send, recv_sem=recv,
            device_id=peer, device_id_type=MESH,
        )

    def rows_of(first, chunk):
        return pl.ds(pl.multiple_of(first + chunk * step, 8), step)

    def at_of(chunk):
        return pl.ds(chunk * step, step)

    def part_copy(at, chunk):
        return remote(
            coef.at[rows_of(slice_of(*offsets[at]), chunk)],
            part_buf.at[at, at_of(chunk)],
            part_send.at[at, chunk],
            part_recv.at[at, chunk],
            block_peer(*offsets[at]),
        )

    def level_copy(bit, chunk):
        return remote(
            run_buf.at[bit - 1, at_of(chunk)],
            pts_buf.at[bit - 1, at_of(chunk)],
            pts_send.at[bit - 1, chunk],
            pts_recv.at[bit - 1, chunk],
            {"pts": pts_peer(bit)},
        )

    def all_copy(at, chunk):
        return remote(
            inc_buf.at[offsets[at][0], at_of(chunk)],
            all_buf.at[at, at_of(chunk)],
            all_send.at[at, chunk],
            all_recv.at[at, chunk],
            block_peer(*offsets[at]),
        )

    def source_rows(at, chunk):
        other, d = offsets[at]
        return rows_of(rep * half + slice_of(other, blk_count - d), chunk)

    def rep_copy(d, at, chunk):
        rows_at = source_rows(at, chunk)
        return remote(
            gather_buf.at[rows_at], gather_buf.at[rows_at],
            rep_send.at[d - 1, at, chunk], rep_recv.at[d - 1, at, chunk],
            {"rep": rep_peer(d)},
        )

    for chunk in range(chunks):
        for at in range(1, len(offsets)):
            part_copy(at, chunk).start()

    def reduce_parts(chunk):
        at = at_of(chunk)
        sums = [coef[rows_of(slice_of(0, 0), chunk), :], None]
        for index in range(1, len(offsets)):
            part_copy(index, chunk).wait_recv()
            got = part_buf[index, at, :]
            other = offsets[index][0]
            sums[other] = got if sums[other] is None else sums[other] + got
        run_buf[0, at, :] = sums[0] + sums[1]
        if levels > 1:
            level_copy(1, chunk).start()
        inc_buf[0, at, :] = sums[1]
        inc_buf[1, at, :] = sums[0]
        if levels == 1:
            share(chunk)

    def level(bit, chunk):
        at = at_of(chunk)
        level_copy(bit, chunk).wait_recv()
        got = pts_buf[bit - 1, at, :]
        if bit + 1 < levels:
            run_buf[bit, at, :] = run_buf[bit - 1, at, :] + got
            level_copy(bit + 1, chunk).start()
        scaled = 2.0 ** (-0.5 * bit) * got
        for other in range(2):
            inc_buf[other, at, :] = inc_buf[other, at, :] + scaled
        if bit + 1 == levels:
            share(chunk)

    def mix(at, chunk, value):
        top = value.astype(jnp.bfloat16)
        rest = value - top.astype(jnp.float32)
        middle = rest.astype(jnp.bfloat16)
        bottom = (rest - middle.astype(jnp.float32)).astype(jnp.bfloat16)
        mats = coupling[...]
        mixed = nt_dot(bottom, mats) + nt_dot(middle, mats) + nt_dot(top, mats)
        gather_buf[source_rows(at, chunk), :] = mixed.astype(jnp.bfloat16).astype(jnp.float32)
        for d in range(1, rep_count):
            rep_copy(d, at, chunk).start()

    def share(chunk):
        for index in range(1, len(offsets)):
            all_copy(index, chunk).start()
        mix(0, chunk, inc_buf[0, at_of(chunk), :])

    def pass_on(chunk):
        for index in range(1, len(offsets)):
            all_copy(index, chunk).wait_recv()
            mix(index, chunk, all_buf[index, at_of(chunk), :])

    for load in loads[3:]:
        load.wait()
    per_core = own_rows // LANES
    own = order_tile[pl.ds(pl.multiple_of(rep * per_core, 8), per_core), :] - start
    own_high = lax.shift_right_logical(own, 7)
    own_low = own & (LANES - 1)
    picked = []
    for axis in range(3):
        value = jnp.zeros((per_core, LANES), jnp.float32)
        for group in range(groups):
            source = jnp.broadcast_to(
                coords[axis : axis + 1, group * LANES : (group + 1) * LANES], (per_core, LANES)
            )
            got = jnp.take_along_axis(source, own_low, axis=1, mode="promise_in_bounds")
            value = jnp.where(own_high == group, got, value)
        picked.append(value)
    blank = jnp.zeros((5, LANES), jnp.float32)
    pieces = []
    for row in range(per_core):
        pieces += [value[row : row + 1] for value in picked] + [blank]
    pieces.append(jnp.zeros((LANES - 8 * per_core, LANES), jnp.float32))
    turned = jnp.concatenate(pieces, axis=0).T
    for row in range(per_core):
        p_cols[row * LANES : (row + 1) * LANES, :] = turned[:, row * 8 : (row + 1) * 8]

    high7 = lax.shift_right_logical(local, 7)
    low7 = local & (LANES - 1)
    leaf_at = lax.broadcasted_iota(jnp.int32, (1, rows), 1) // LEAF
    key = leaf_at * groups + high7
    left = lax.broadcasted_iota(jnp.int32, (leaf_count * groups, rows), 0) == key
    right = lax.broadcasted_iota(jnp.int32, (LANES, rows), 0) == low7
    member = nt_dot(
        jnp.where(left, 1.0, 0.0).astype(jnp.bfloat16),
        jnp.where(right, 1.0, 0.0).astype(jnp.bfloat16),
    )
    folded = [
        jnp.concatenate(
            [coords[axis : axis + 1, g * LANES : (g + 1) * LANES] for g in range(groups)], axis=0
        )
        for axis in range(3)
    ]
    for own_leaf in range(own_leaves):
        entries = near_list[pl.ds(rep * own_leaves + own_leaf, 1), :] - base_leaf
        live = jnp.zeros((groups, LANES), jnp.float32)
        for other in range(leaf_count):
            hit = jnp.where(entries == other, 1.0, 0.0)
            weight = jnp.sum(hit, axis=1, keepdims=True)
            live = live + weight * member[other * groups : (other + 1) * groups]
        q_rows[own_leaf * groups : (own_leaf + 1) * groups, :] = jnp.where(
            live > 0.5, folded[0], FAR_AWAY
        )
    for axis in (1, 2):
        at = (own_leaves + axis - 1) * groups
        q_rows[at : at + groups, :] = folded[axis]

    def near_tile(tile):
        leaf = tile * TILE // LEAF
        for sub in range(TILE // SUB):
            at = tile * TILE + sub * SUB
            left = [
                jnp.broadcast_to(p_cols[at : at + SUB, axis : axis + 1], (SUB, LANES))
                for axis in range(3)
            ]
            for group in range(groups):
                gap = []
                for axis in range(3):
                    row = (leaf if axis == 0 else own_leaves + axis - 1) * groups + group
                    gap.append(left[axis] - q_rows[row : row + 1, :])
                dist = gap[0] * gap[0] + gap[1] * gap[1] + gap[2] * gap[2]
                k_buf[sub * SUB : (sub + 1) * SUB, group * LANES : (group + 1) * LANES] = jnp.exp(
                    -dist * spread
                ).astype(jnp.bfloat16)
        near_buf[tile] = jnp.dot(
            k_buf[...], x_buf[...], preferred_element_type=jnp.float32
        ) * (LEAF ** -0.5)
        near_copy(tile).start()

    def near_copy(tile):
        return pltpu.make_async_copy(
            near_buf.at[tile], near_out.at[pl.ds(tile * TILE, TILE)], near_sem.at[tile]
        )

    stages = [reduce_parts]
    stages += [functools.partial(level, bit) for bit in range(1, levels)]
    stages.append(pass_on)
    lag = chunks
    tile_at = 0
    for wave in range(chunks + lag * (len(stages) - 1)):
        for _ in range(near_waves.count(wave)):
            if tile_at < own_rows // TILE:
                near_tile(tile_at)
                tile_at += 1
        for at, stage in enumerate(stages):
            chunk = wave - lag * at
            if 0 <= chunk < chunks:
                stage(chunk)
    for tile in range(tile_at, own_rows // TILE):
        near_tile(tile)
    for chunk in range(chunks):
        for at in range(len(offsets)):
            for d in range(1, rep_count):
                rep_copy(d, at, chunk).wait_recv()
    mixed_out[...] = gather_buf[...].astype(jnp.bfloat16)
    for chunk in range(chunks):
        for at in range(len(offsets)):
            if at:
                part_copy(at, chunk).wait_send()
                all_copy(at, chunk).wait_send()
            for d in range(1, rep_count):
                rep_copy(d, at, chunk).wait_send()
        for bit in range(1, levels):
            level_copy(bit, chunk).wait_send()
    for tile in range(own_rows // TILE):
        near_copy(tile).wait()


def finish_kernel(mixed, near, panels, out_hbm, buf, out_sem):
    tiles = buf.shape[0]
    rep = lax.axis_index("rep")
    stores = []
    for tile in range(tiles):
        at = pl.ds(tile * TILE, TILE)
        own = pl.ds(pl.multiple_of((rep * tiles + tile) * TILE, TILE), TILE)
        buf[tile] = near[at, :] + nt_dot(panels[own, :], mixed[...])
        stores.append(pltpu.make_async_copy(buf.at[tile], out_hbm.at[at], out_sem.at[tile]))
        stores[-1].start()
    for store in stores:
        store.wait()


def on_device(points_x, coords, panels, coupling, near_list, order):
    rows, nrhs = points_x.shape
    rank = panels.shape[1]
    blk_count = lax.axis_size("blk")
    rep_count = lax.axis_size("rep")
    levels = min(lax.axis_size("pts").bit_length() - 1, 4)
    half = nrhs // rep_count
    piece = half // (2 * blk_count)
    own_rows = rows // rep_count
    tiles = own_rows // TILE
    groups = rows // LANES
    own_leaves = own_rows // LEAF
    chunks = CHUNKS
    slots = max(levels - 1, 1)
    members = 2 * blk_count
    vmem = pl.BlockSpec(memory_space=pltpu.VMEM)
    any_space = pl.BlockSpec(memory_space=pl.ANY)
    dma = pltpu.SemaphoreType.DMA
    f32 = jnp.float32
    bf16 = jnp.bfloat16

    operands = (
        order.reshape(1, rows), order.reshape(groups, LANES), coords, near_list, panels, coupling, points_x
    )
    near, mixed = pl.pallas_call(
        functools.partial(exchange_kernel, levels, chunks, NEAR_WAVES),
        out_shape=(
            jax.ShapeDtypeStruct((own_rows, nrhs), f32),
            jax.ShapeDtypeStruct((nrhs, rank), bf16),
        ),
        in_specs=[pl.BlockSpec(memory_space=pltpu.HBM)] * 7,
        out_specs=(any_space, vmem),
        scratch_shapes=[
            pltpu.VMEM((1, rows), jnp.int32),
            pltpu.VMEM((groups, LANES), jnp.int32),
            pltpu.VMEM((3, rows), f32),
            pltpu.VMEM(near_list.shape, jnp.int32),
            pltpu.VMEM((rows, rank), bf16),
            pltpu.VMEM((rank, rank), bf16),
            pltpu.VMEM((rows, nrhs), bf16),
            pltpu.VMEM((own_rows, 8), f32),
            pltpu.VMEM(((own_leaves + 2) * groups, LANES), f32),
            pltpu.VMEM((half, rank), f32),
            pltpu.VMEM((TILE, rows), bf16),
            pltpu.VMEM((tiles, TILE, nrhs), f32),
            pltpu.VMEM((members, piece, rank), f32),
            pltpu.VMEM((slots, piece, rank), f32),
            pltpu.VMEM((slots, piece, rank), f32),
            pltpu.VMEM((2, piece, rank), f32),
            pltpu.VMEM((members, piece, rank), f32),
            pltpu.VMEM((nrhs, rank), f32),
            dma((7,)),
            dma((tiles,)),
            dma((members, chunks)),
            dma((members, chunks)),
            dma((slots, chunks)),
            dma((slots, chunks)),
            dma((members, chunks)),
            dma((members, chunks)),
            dma((rep_count - 1, members, chunks)),
            dma((rep_count - 1, members, chunks)),
        ],
        compiler_params=pltpu.CompilerParams(
            collective_id=0, has_side_effects=True, vmem_limit_bytes=VMEM_MIB * 2**20
        ),
        name="exchange",
    )(*[pltpu.with_memory_space_constraint(value, pltpu.HBM) for value in operands])

    return pl.pallas_call(
        finish_kernel,
        out_shape=jax.ShapeDtypeStruct((own_rows, nrhs), f32),
        in_specs=[vmem, vmem, vmem],
        out_specs=any_space,
        scratch_shapes=[
            pltpu.VMEM((tiles, TILE, nrhs), f32),
            dma((tiles,)),
        ],
        compiler_params=pltpu.CompilerParams(vmem_limit_bytes=32 * 2**20),
        name="finish",
    )(mixed, near, panels)


def solution(mesh):
    placed = (
        P(("groups", "pts", "blk"), None),
        P(None, ("groups", "pts", "blk")),
        P(("groups", "pts", "blk"), None),
        P(("groups", "pts"), None),
        P(("groups", "pts", "blk"), None),
        P(("groups", "pts", "blk")),
    )
    return jax.shard_map(
        on_device,
        mesh=mesh,
        in_specs=placed,
        out_specs=P(("groups", "pts", "blk", "rep"), None),
        check_vma=False,
    )
```
